32 devices in a mesh: row: 8 (over z, core), col: 4 (over y, x).
Axes of the slice: x: 2, y: 2, z: 4, core: 2. Of those that a mesh axis runs over, the one named last changes fastest.
Arguments:
- stored: bfloat16 [1024, 51200], P(('row', 'col')), may hold values from -6 to 6
- integrals: bfloat16 [51200, 25600], P('row', 'col'), may hold values from -0.02734375 to 0.02734375
- layout: int32 [1024], replicated, may hold values from 0 to 1023, each once
- partner: int32 [1024], replicated, may hold values from 0 to 1023, as said below
Outputs:
- residual_out: bfloat16 [1024, 25600], P('row', 'col')
The draws below stay inside these ranges and needn't reach their ends.
Inputs may be any that keep to these rules, and one draw needn't show every extreme that they name: partner is an involution without fixed points: partner[p] != p and partner[partner[p]] = p. `layout`: each slab pair stands in exactly one stored row.
All inputs are finite; a program needn't handle non-finite values.
Results may differ from the reference program's by a relative error of at most 0.001.
Values may be sent and summed in bfloat16 or wider, within the bound.
No kernel may reach another device: no remote copies, remote signals or barrier semaphores. Data moves between devices by JAX's collectives and lax.ppermute only.
A program may use at most 256 MiB of HBM per device.

```python
import jax
import jax.numpy as jnp
from jax import lax

NV = 1600
AW = 16
P_SIZE = 1024
K = 51200
N = 25600


def draw_partner(key, part):
    order = jax.random.permutation(key, jnp.arange(P_SIZE, dtype=jnp.int32))
    firsts = order[0::2]
    seconds = order[1::2]
    coupled = jnp.zeros((P_SIZE,), jnp.int32).at[firsts].set(seconds)
    return coupled.at[seconds].set(firsts)


def spiked(result, key, source, target, shards_of, factor):
    owner, partner = [(jnp.arange(result.shape[dim]) // (result.shape[dim] // shards_of)).reshape([-1 if axis == dim else 1 for axis in range(result.ndim)]) for dim in (source, target)]
    chosen = jax.random.permutation(key, shards_of)[partner]
    strong = (owner == chosen) | (owner == (partner + shards_of // 2) % shards_of)
    return jnp.where(strong, factor * result, result)


def levels(stream_key, dims, shards, smallest, top_value):
    def one(axis_at, blocks):
        steps = jax.random.uniform(jax.random.fold_in(jax.random.fold_in(stream_key, 6), axis_at), (blocks,), jnp.float32, smallest / len(shards), top_value / len(shards))
        return jnp.repeat(jnp.exp(steps), dims[axis_at] // blocks).reshape((-1,) + (1,) * (len(dims) - axis_at - 1))

    gain = one(*shards[0])
    for cut in shards[1:]:
        gain = gain * one(*cut)
    return gain


def noise(own_key, dims, deviation, bound, cuts=(), kind=jnp.bfloat16):
    result = deviation * jax.random.normal(own_key, dims, jnp.float32)
    if cuts:
        result = result * levels(own_key, dims, cuts, -0.22, 0.18)
    return jnp.clip(result, -bound, bound).astype(kind)


def bell_draw_with(stream_key, dims, deviation, most, split, heavy, kind=jnp.bfloat16):
    result = deviation * jax.random.normal(stream_key, dims, jnp.float32)
    if split:
        result = result * levels(stream_key, dims, split, -0.22, 0.18)
    return jnp.clip(spiked(result, jax.random.fold_in(stream_key, 3), *heavy), -most, most).astype(kind)


def setup_inputs(seed: int = 0) -> dict:
    streams_of = jax.random.split(jax.random.key(seed), 5)
    stored = bell_draw_with(streams_of[0], (P_SIZE, K), 1.0, 6.0, ((0, 32),), (1, 0, 32, 2.75))
    integrals = noise(streams_of[1], (K, N), K ** -0.5, 0.02734375, ((0, 8), (1, 4)))
    layout = jax.random.permutation(streams_of[2], P_SIZE).astype(jnp.int32)
    partner = draw_partner(jax.random.fold_in(streams_of[4], 71), 0)
    return dict(stored=stored, integrals=integrals, layout=layout, partner=partner)


def reference(stored, integrals, layout, partner):
    amplitudes = jnp.zeros_like(stored).at[layout].set(stored)

    def one_block(block_index):
        columns = lax.dynamic_slice_in_dim(integrals, block_index * NV, NV, 1)
        return jnp.dot(amplitudes, columns, preferred_element_type=jnp.float32)

    blocks = lax.map(one_block, jnp.arange(AW, dtype=jnp.int32))
    ladder = jnp.transpose(blocks, (1, 0, 2)).reshape(P_SIZE, AW * NV)
    return (ladder - ladder[partner]).astype(jnp.bfloat16)
```

```python
import functools

import jax
import jax.numpy as jnp
import numpy as np
from jax import lax
from jax.experimental import pallas as pl
from jax.experimental.pallas import tpu as pltpu
from jax.sharding import PartitionSpec as P

F32, BF16, F8, I16, I32 = jnp.float32, jnp.bfloat16, jnp.float8_e4m3fn, jnp.int16, jnp.int32
UNITS = 25
CHUNKS = (6, 9, 10)
WIDE = 5
GROUPS = (2, 3)
PARTS = ((0, 0, 5), (0, 5, 5), (1, 0, 5), (1, 5, 5), (1, 10, 5))
EXTRA = 16
MIB = 1024 * 1024
COST = 1
ORDER = (
    (0, 0), (1, 0), (2, 0), (0, 1), (3, 0), (2, 1), (1, 1), (2, 2), (2, 3), (3, 1), (2, 4), (4, 0), (3, 2), (5, 0), (4, 1),
    (3, 3), (5, 1), (4, 2), (3, 4), (5, 2), (4, 3), (5, 3), (4, 4), (5, 4),
)


def in_place(ref_rows, width):
    return pl.BlockSpec((ref_rows, width), lambda n, *_: (0, n))


class Chain:
    def __init__(self):
        self.mark = None

    def call(
        self, body, arrays, in_specs, out_specs, out_shape, grid, scalars=None, vmem=16, cost=COST, scratch_shapes=(), **kw
    ):
        marks = [] if self.mark is None else [self.mark]
        n_scalars, n_in, n_out, n_marks = scalars is not None, len(arrays), len(out_shape), len(marks)

        def wrapped(*refs):
            ahead, rest = refs[:n_scalars], refs[n_scalars:]
            outs, scratch = rest[n_in + n_marks :][:n_out], rest[n_in + n_marks + n_out + 1 :]
            body(*ahead, *rest[:n_in], *outs, *scratch)
            mark = rest[n_in + n_marks + n_out]
            mark[...] = jnp.zeros_like(mark)

        anywhere = pl.BlockSpec(memory_space=pl.ANY)
        *outs, self.mark = pl.pallas_call(
            wrapped,
            grid_spec=pltpu.PrefetchScalarGridSpec(
                num_scalar_prefetch=n_scalars,
                grid=grid,
                in_specs=[*in_specs, *[anywhere] * n_marks],
                out_specs=[*out_specs, pl.BlockSpec((8, 128), lambda *_: (0, 0))],
                scratch_shapes=scratch_shapes,
            ),
            out_shape=[*out_shape, jax.ShapeDtypeStruct((8, 128), F32)],
            compiler_params=pltpu.CompilerParams(vmem_limit_bytes=vmem * MIB),
            cost_estimate=pl.CostEstimate(flops=cost, bytes_accessed=cost, transcendentals=0),
            **kw,
        )(*([scalars] if n_scalars else []), *arrays, *marks)
        return outs


def split_body(place_ref, *refs):
    for i, ref in enumerate(refs[:-1]):
        refs[-1][i] = ref[...]


def join_body(*refs):
    count = len(refs) // 3
    for i in range(count):
        rows = refs[2 * i].shape[0]
        refs[2 * count + i][0:rows, :] = refs[2 * i][...]
        refs[2 * count + i][rows:, :] = refs[2 * i + 1][...]


def stack_body(line, with_halves, with_pieces):
    def body(place_ref, *refs):
        refs = list(refs)
        pieces = [refs.pop(0) for _ in range(line * with_halves)]
        own = [refs.pop(0) for _ in range(line * with_pieces)]
        other = [refs.pop(0) for _ in range(line * with_pieces)]
        halves = [refs.pop(0) for _ in range(2 * with_halves)]
        for i, ref in enumerate(pieces):
            rows, at = ref.shape[0], i % (line // 2)
            halves[i // (line // 2)][at * rows : (at + 1) * rows, :] = ref[...]
        for first, second, target in zip(own, other, refs):
            rows = first.shape[0]
            target[0:rows, :] = first[...]
            target[rows:, :] = second[...]

    return body


def pair_rows_body(select_ref, *refs):
    *piece_refs, high_ref, low_ref, scale_ref = refs
    at = pl.program_id(0)

    @pl.when(at == 0)
    def _():
        tops = [jnp.max(jnp.abs(ref[...]), axis=0, keepdims=True) for ref in piece_refs]
        top = jnp.max(functools.reduce(jnp.maximum, tops).astype(F32), axis=1, keepdims=True)
        scale_ref[...] = jnp.broadcast_to(jnp.maximum(top, 1e-30) * (2.0**-7 / 440.0), scale_ref.shape)

    width = high_ref.shape[1]
    here = pl.ds(pl.multiple_of(at * width, width), width)
    rows = jnp.concatenate([ref[:, here] for ref in piece_refs], axis=0)
    diff = jnp.dot(select_ref[...], rows, preferred_element_type=F32)
    high = diff.astype(BF16)
    high_ref[...] = high
    low_ref[...] = ((diff - high.astype(F32)) * (1.0 / scale_ref[0:1, 0:1])).astype(F8)


def product(high_ref, low_ref, scale_ref, block_ref):
    block = block_ref[...]
    value = jnp.dot(high_ref[...], block, preferred_element_type=F32)
    top = jnp.maximum(jnp.max(jnp.abs(block), axis=0, keepdims=True).astype(F32), 1e-30)
    small = (block * (440.0 / top).astype(BF16)).astype(F8)
    low = jnp.dot(low_ref[...], small, preferred_element_type=F32)
    return value + low * scale_ref[0:1, 0:1] * (1.0 / (440.0 / top).astype(BF16).astype(F32))


def first_body(high_ref, low_ref, scale_ref, block_ref, out_ref):
    out_ref[...] = product(high_ref, low_ref, scale_ref, block_ref)


def middle_body(high_ref, low_ref, scale_ref, block_ref, sum_ref, out_ref):
    out_ref[...] = sum_ref[...] + product(high_ref, low_ref, scale_ref, block_ref)


def last_body(high_ref, low_ref, scale_ref, block_ref, sum_ref, own_ref, other_ref):
    value = sum_ref[...] + product(high_ref, low_ref, scale_ref, block_ref)
    half = value.shape[0] // 2
    own_ref[...] = value[:half]
    other_ref[...] = value[half:]


def encode(value, out_ref):
    rows = value.shape[0]
    top = jnp.maximum(jnp.max(jnp.abs(value), axis=0, keepdims=True), 1e-30)
    step = jnp.ceil(16.0 * jnp.log2(top * (1.0 / 32700.0)))
    inverse = jnp.exp2(step * (-1.0 / 16.0))
    fixed = jnp.clip(jnp.round(value * inverse), -32767.0, 32767.0)
    out_ref[0:rows, :] = fixed.astype(I32).astype(I16)
    out_ref[rows:, :] = jnp.broadcast_to(step, (EXTRA, value.shape[1])).astype(I32).astype(I16)


def decode(ref):
    rows = ref.shape[0] - EXTRA
    step = ref[rows:, :].astype(I32).astype(F32)[0:1, :]
    return ref[0:rows, :].astype(I32).astype(F32) * jnp.exp2(step * (1.0 / 16.0))


def add_plain_body(a_ref, b_ref, sum_ref, code_ref):
    value = a_ref[...] + b_ref[...]
    sum_ref[...] = value
    encode(value, code_ref)


def add_coded_body(a_ref, code_in_ref, sum_ref, code_ref):
    value = a_ref[...] + decode(code_in_ref)
    sum_ref[...] = value
    encode(value, code_ref)


def add_last_body(a_ref, code_in_ref, out_ref):
    out_ref[...] = (a_ref[...] + decode(code_in_ref)).astype(BF16)


def pick_body(pick_ref, own_ref, other_ref, out_ref, far_ref):
    half = own_ref.shape[0]
    near = out_ref.shape[0]
    value = jnp.dot(pick_ref[:, 0:half], own_ref[...], preferred_element_type=F32)
    value += jnp.dot(pick_ref[:, half:], other_ref[...], preferred_element_type=F32)
    out_ref[...] = value[:near].astype(BF16)
    far_ref[...] = value[near:].astype(BF16)


def per_device(stored, integrals, layout, partner):
    rows = stored.shape[0]
    n_row, n_col = lax.axis_size("row"), lax.axis_size("col")
    line = n_row // 2
    total = rows * n_row * n_col
    pairs = total // 2
    half = pairs // 2
    depth, columns = integrals.shape
    unit, tile = depth // UNITS, columns // UNITS
    r, c = lax.axis_index("row"), lax.axis_index("col")
    z, core = r // 2, r % 2
    place = jnp.stack([z, core]).astype(I32)
    siblings = [(i, i ^ 1) for i in range(n_row)]
    chain = Chain()
    starts = [sum(CHUNKS[:i]) for i in range(len(CHUNKS))]

    def split():
        def at(i):
            return lambda u, p: (0, 2 * i + 1 - p[1])

        return chain.call(
            split_body,
            [stored] * line,
            [pl.BlockSpec((rows, depth), at(i)) for i in range(line)],
            [pl.BlockSpec((line, rows, depth), lambda u, p: (0, 0, 0))],
            [jax.ShapeDtypeStruct((line, rows, depth), BF16)],
            (1,),
            scalars=place,
        )[0]

    def stack(pieces, following):
        def whole(shape):
            return pl.BlockSpec(shape, lambda u, p: (0, 0))

        def at(step):
            return lambda u, p: (0, ((2 * lax.rem(p[0] + step, line) + p[1]) * UNITS + starts[following]) * unit)

        def other_at(step):
            return lambda u, p: (lax.rem(p[0] + step, line), 0, starts[following] * unit)

        arrays, in_specs, shapes = [], [], []
        if pieces is not None:
            rows_of, width = pieces[0].shape
            arrays += pieces
            in_specs += [whole((rows_of, width))] * line
            shapes += [(rows_of * line // 2, width)] * 2
        if following is not None:
            width = CHUNKS[following] * unit
            arrays += [stored] * line + [others] * line
            in_specs += [pl.BlockSpec((pl.Element(rows), pl.Element(width)), at(s)) for s in range(line)]
            in_specs += [pl.BlockSpec((None, pl.Element(rows), pl.Element(width)), other_at(s)) for s in range(line)]
            shapes += [(2 * rows, width)] * line
        outs = chain.call(
            stack_body(line, pieces is not None, following is not None),
            arrays,
            in_specs,
            [whole(shape) for shape in shapes],
            [jax.ShapeDtypeStruct(shape, BF16) for shape in shapes],
            (1,),
            scalars=place,
        )
        halves = outs[:2] if pieces is not None else None
        return halves, outs[2 if pieces is not None else 0 :]

    def along_z(pieces):
        out = pieces[:1]
        for step in range(1, line):
            perm = [(2 * i + k, 2 * ((i + step) % line) + k) for i in range(line) for k in range(2)]
            out.append(lax.ppermute(pieces[step], "row", perm))
        return out

    bits = [1 << b for b in range(n_col.bit_length() - 1)]
    orders = [bits, bits[::-1]]

    def over_col(halves):
        have = [[h] for h in halves]
        joined = halves
        for i in range(len(bits)):
            if i:
                width = joined[0].shape[1]
                grown = 2 * joined[0].shape[0]
                specs = [pl.BlockSpec((grown // 2, width), lambda u: (0, 0))] * 4
                joined = chain.call(
                    join_body,
                    [x for h in range(2) for x in (joined[h], have[h][-1])],
                    specs,
                    [pl.BlockSpec((grown, width), lambda u: (0, 0))] * 2,
                    [jax.ShapeDtypeStruct((grown, width), BF16)] * 2,
                    (1,),
                    vmem=32,
                )
            for h in range(2):
                perm = [(x, x ^ orders[h][i]) for x in range(n_col)]
                have[h].append(lax.ppermute(joined[h], "col", perm))
            yield
        return have[0] + have[1]

    def pair_rows(chunk, pieces):
        width = CHUNKS[chunk] * unit
        shapes = [((pairs, width), BF16), ((pairs, width), F8), ((8, 128), F32)]
        return chain.call(
            pair_rows_body,
            [select, *pieces],
            [pl.BlockSpec((pairs, total), lambda n: (0, 0))] + [pl.BlockSpec(p.shape, lambda n: (0, 0)) for p in pieces],
            [in_place(pairs, unit), in_place(pairs, unit), pl.BlockSpec((8, 128), lambda n: (0, 0))],
            [jax.ShapeDtypeStruct(shape, kind) for shape, kind in shapes],
            (CHUNKS[chunk],),
            vmem=32,
        )

    wide = WIDE * tile

    def product_specs(chunk, diff, first):
        rows_of = CHUNKS[chunk] * unit
        return [
            *[pl.BlockSpec(d.shape, lambda n: (0, 0)) for d in diff],
            pl.BlockSpec(
                (pl.Element(rows_of), pl.Element(wide)), lambda n: (starts[chunk] * unit, (first + n) * wide)
            ),
        ]

    def accumulate(chunk, diff, sums):
        in_specs = product_specs(chunk, diff, 0)
        kw = dict(
            out_specs=[in_place(pairs, wide)],
            out_shape=[jax.ShapeDtypeStruct((pairs, columns), F32)],
            grid=(columns // wide,),
            vmem=56,
        )
        if sums is None:
            return chain.call(first_body, [*diff, integrals], in_specs, **kw)[0]
        return chain.call(
            middle_body,
            [*diff, integrals, sums],
            [*in_specs, in_place(pairs, wide)],
            input_output_aliases={4: 0},
            **kw,
        )[0]

    def finish(group, diff, sums):
        first = sum(GROUPS[:group])
        return chain.call(
            last_body,
            [*diff, integrals, sums],
            [*product_specs(n - 1, diff, first), pl.BlockSpec((pairs, wide), lambda n: (0, first + n))],
            [in_place(half, wide)] * 2,
            [jax.ShapeDtypeStruct((half, GROUPS[group] * wide), F32)] * 2,
            (GROUPS[group],),
            vmem=56,
        )

    def by_columns(body, arrays, outs, first=0, units=None):
        count = arrays[-1].shape[1] // tile if units is None else units
        return chain.call(
            body,
            arrays,
            [pl.BlockSpec((a.shape[0], tile), lambda n: (0, first + n)) for a in arrays],
            [in_place(rows_of, tile) for rows_of, _ in outs],
            [jax.ShapeDtypeStruct((rows_of, count * tile), kind) for rows_of, kind in outs],
            (count,),
        )

    def row_ids():
        entries = []
        for h in range(2):
            masks = [0]
            for bit in orders[h]:
                masks += [m ^ bit for m in masks]
            for m in masks:
                for step in range(h * line // 2, (h + 1) * line // 2):
                    for flip in range(2):
                        entries += [(m, step, flip, offset) for offset in range(rows)]
        mask, step, flip, offset = np.array(entries, np.int32).T
        return ((2 * ((z - step) % line) + (core ^ flip)) * n_col + (c ^ mask)) * rows + offset

    n = len(CHUNKS)
    others = lax.ppermute(split(), "row", siblings)
    _, pieces = stack(None, 0)
    pieces = along_z(pieces)

    slab = jnp.arange(total, dtype=I32) + chain.mark[0, 0].astype(I32)
    is_first = slab < partner
    before = is_first[None, :] & (slab[None, :] < jnp.minimum(slab, partner)[:, None])
    number = jnp.sum(before.astype(I32), axis=1) + 1
    signed = jnp.where(is_first, number, -number)
    held = jnp.sum(jnp.where(slab[None, :] == layout[:, None], signed[None, :], 0), axis=1)
    held = jnp.sum(jnp.where(slab[None, :] == row_ids()[:, None], held[None, :], 0), axis=1)
    order = (jnp.arange(pairs, dtype=I32) + core * half) % pairs + 1
    select = (order[:, None] == held[None, :]).astype(BF16) - (order[:, None] == -held[None, :]).astype(BF16)
    middle = line // 2
    mine_rows = total // n_row
    outward = jnp.where(z < middle, -1, 1)
    owners = jnp.clip(z + outward * np.arange(middle, dtype=np.int32), 0, line - 1)
    wanted = (2 * jnp.repeat(owners, mine_rows) + core) * mine_rows + np.tile(np.arange(mine_rows, dtype=np.int32), middle)
    mine = jnp.sum(jnp.where(slab[None, :] == wanted[:, None], signed[None, :], 0), axis=1)
    pick = (mine[:, None] == order[None, :]).astype(BF16) - (mine[:, None] == -order[None, :]).astype(BF16)

    sums = None

    def advance(exchange):
        try:
            next(exchange)
        except StopIteration as end:
            return end.value

    halves, pieces = stack(pieces, 1)
    pieces = along_z(pieces)
    exchange = over_col(halves)
    blocks = None
    while blocks is None:
        blocks = advance(exchange)
    for i in range(1, n):
        halves, pieces = following if i > 1 else stack(pieces, i + 1 if i + 1 < n else None)
        if i + 1 < n:
            pieces = along_z(pieces)
        exchange = over_col(halves)
        advance(exchange)
        diff = pair_rows(i - 1, blocks)
        blocks = None
        while blocks is None:
            blocks = advance(exchange)
        sums = accumulate(i - 1, diff, sums)
        if i + 1 < n:
            following = stack(pieces, i + 2 if i + 2 < n else None)
    diff = pair_rows(n - 1, blocks)

    def along(pairs_of_z):
        return [(2 * a + k, 2 * b + k) for a, b in pairs_of_z for k in range(2)]

    groups = [None] * len(GROUPS)

    def send(group):
        own, foreign = groups[group]
        anywhere = pl.BlockSpec(memory_space=pl.ANY)
        shape = jax.ShapeDtypeStruct(foreign.shape, foreign.dtype)
        (foreign,) = chain.call(
            lambda *refs: None, [foreign], [anywhere], [anywhere], [shape], (1,), input_output_aliases={0: 0}
        )
        groups[group] = [own, lax.ppermute(foreign, "row", siblings)]

    def begin(part):
        group, first, units = PARTS[part]
        return groups[group], first, units

    def inward(step, state):
        outs = [(half, F32), (half + EXTRA, I16)]
        if step == 0:
            value, code = by_columns(add_plain_body, state[0], outs, state[1], state[2])
        else:
            value, code = by_columns(add_coded_body, list(state), outs)
        if step < middle - 1:
            perm = along([(step, step + 1), (line - 1 - step, line - 2 - step)])
        else:
            perm = along([(middle - 1, middle), (middle, middle - 1)])
        return value, lax.ppermute(code, "row", perm)

    def whole(state):
        (done,) = by_columns(add_last_body, list(state), [(half, BF16)])
        return done, lax.ppermute(done, "row", siblings)

    def spread(state):
        width = state[0].shape[1]
        far = (middle - 1) * mine_rows
        own, rest = chain.call(
            pick_body,
            [pick, *state],
            [pl.BlockSpec(pick.shape, lambda n: (0, 0)), in_place(half, tile), in_place(half, tile)],
            [in_place(mine_rows, tile), in_place(far, tile)],
            [jax.ShapeDtypeStruct((mine_rows, width), BF16), jax.ShapeDtypeStruct((far, width), BF16)],
            (width // tile,),
        )
        distance = jnp.where(z < middle, middle - 1 - z, z - middle)
        for step in range(middle - 1):
            perm = along([(middle - 1 - step, middle - 2 - step), (middle + step, middle + 1 + step)])
            rest = lax.ppermute(rest, "row", perm)
            own = jnp.where(distance == step + 1, rest[:mine_rows], own)
            rest = rest[mine_rows:]
        return own

    stages = [lambda s, k=k: inward(k, s) for k in range(middle)] + [whole, spread]
    state = [None] * len(PARTS)
    for stage, item in ORDER if len(stages) == 4 else (
        [(k, g) for k in (0, 1) for g in range(len(GROUPS))]
        + sorted(
            ((k + 2, p) for p in range(len(PARTS)) for k in range(len(stages))), key=lambda x: (x[0] + x[1], x[0])
        )
    ):
        if stage == 0:
            groups[item] = finish(item, diff, sums)
        elif stage == 1:
            send(item)
        else:
            state[item] = stages[stage - 2](begin(item) if stage == 2 else state[item])
    return jnp.concatenate(state, axis=1)


def solution(mesh):
    return jax.shard_map(
        per_device,
        mesh=mesh,
        in_specs=(P(("row", "col"), None), P("row", "col"), P(), P()),
        out_specs=P("row", "col"),
        check_vma=False,
    )
```

```python
import functools

import jax
import jax.numpy as jnp
import numpy as np
from jax import lax
from jax.experimental import pallas as pl
from jax.experimental.pallas import tpu as pltpu
from jax.sharding import PartitionSpec as P

F32, BF16, F8, I16, I32 = jnp.float32, jnp.bfloat16, jnp.float8_e4m3fn, jnp.int16, jnp.int32
UNITS = 25
CHUNKS = (6, 9, 10)
WIDE = 5
GROUPS = (2, 3)
PARTS = ((0, 0, 5), (0, 5, 5), (1, 0, 5), (1, 5, 5), (1, 10, 5))
EXTRA = 16
MIB = 1024 * 1024
COST = 1
ORDER = (
    (0, 0), (1, 0), (2, 0), (2, 1), (0, 1), (3, 0), (3, 1), (1, 1), (2, 2), (2, 3), (2, 4), (4, 0), (4, 1), (3, 2), (5, 0),
    (3, 3), (5, 1), (4, 2), (3, 4), (5, 2), (4, 3), (5, 3), (4, 4), (5, 4),
)


def in_place(ref_rows, width):
    return pl.BlockSpec((ref_rows, width), lambda n, *_: (0, n))


class Chain:
    def __init__(self):
        self.mark = None

    def call(
        self, body, arrays, in_specs, out_specs, out_shape, grid, scalars=None, vmem=16, cost=COST, scratch_shapes=(), **kw
    ):
        marks = [] if self.mark is None else [self.mark]
        n_scalars, n_in, n_out, n_marks = scalars is not None, len(arrays), len(out_shape), len(marks)

        def wrapped(*refs):
            ahead, rest = refs[:n_scalars], refs[n_scalars:]
            outs, scratch = rest[n_in + n_marks :][:n_out], rest[n_in + n_marks + n_out + 1 :]
            body(*ahead, *rest[:n_in], *outs, *scratch)
            mark = rest[n_in + n_marks + n_out]
            mark[...] = jnp.zeros_like(mark)

        anywhere = pl.BlockSpec(memory_space=pl.ANY)
        *outs, self.mark = pl.pallas_call(
            wrapped,
            grid_spec=pltpu.PrefetchScalarGridSpec(
                num_scalar_prefetch=n_scalars,
                grid=grid,
                in_specs=[*in_specs, *[anywhere] * n_marks],
                out_specs=[*out_specs, pl.BlockSpec((8, 128), lambda *_: (0, 0))],
                scratch_shapes=scratch_shapes,
            ),
            out_shape=[*out_shape, jax.ShapeDtypeStruct((8, 128), F32)],
            compiler_params=pltpu.CompilerParams(vmem_limit_bytes=vmem * MIB),
            cost_estimate=pl.CostEstimate(flops=cost, bytes_accessed=cost, transcendentals=0),
            **kw,
        )(*([scalars] if n_scalars else []), *arrays, *marks)
        return outs


def split_body(place_ref, *refs):
    for i, ref in enumerate(refs[:-1]):
        refs[-1][i] = ref[...]


def join_body(*refs):
    count = len(refs) // 3
    for i in range(count):
        rows = refs[2 * i].shape[0]
        refs[2 * count + i][0:rows, :] = refs[2 * i][...]
        refs[2 * count + i][rows:, :] = refs[2 * i + 1][...]


def stack_body(line, with_halves, with_pieces):
    def body(place_ref, *refs):
        refs = list(refs)
        pieces = [refs.pop(0) for _ in range(line * with_halves)]
        own = [refs.pop(0) for _ in range(line * with_pieces)]
        other = [refs.pop(0) for _ in range(line * with_pieces)]
        halves = [refs.pop(0) for _ in range(2 * with_halves)]
        for i, ref in enumerate(pieces):
            rows, at = ref.shape[0], i % (line // 2)
            halves[i // (line // 2)][at * rows : (at + 1) * rows, :] = ref[...]
        for first, second, target in zip(own, other, refs):
            rows = first.shape[0]
            target[0:rows, :] = first[...]
            target[rows:, :] = second[...]

    return body


def pair_rows_body(select_ref, *refs):
    *piece_refs, high_ref, low_ref, scale_ref = refs
    at = pl.program_id(0)

    @pl.when(at == 0)
    def _():
        tops = [jnp.max(jnp.abs(ref[...]), axis=0, keepdims=True) for ref in piece_refs]
        top = jnp.max(functools.reduce(jnp.maximum, tops).astype(F32), axis=1, keepdims=True)
        scale_ref[...] = jnp.broadcast_to(jnp.maximum(top, 1e-30) * (2.0**-7 / 440.0), scale_ref.shape)

    width = high_ref.shape[1]
    here = pl.ds(pl.multiple_of(at * width, width), width)
    rows = jnp.concatenate([ref[:, here] for ref in piece_refs], axis=0)
    diff = jnp.dot(select_ref[...], rows, preferred_element_type=F32)
    high = diff.astype(BF16)
    high_ref[...] = high
    low_ref[...] = ((diff - high.astype(F32)) * (1.0 / scale_ref[0:1, 0:1])).astype(F8)


def product(high_ref, low_ref, scale_ref, block_ref):
    block = block_ref[...]
    value = jnp.dot(high_ref[...], block, preferred_element_type=F32)
    top = jnp.maximum(jnp.max(jnp.abs(block), axis=0, keepdims=True).astype(F32), 1e-30)
    small = (block * (440.0 / top).astype(BF16)).astype(F8)
    low = jnp.dot(low_ref[...], small, preferred_element_type=F32)
    return value + low * scale_ref[0:1, 0:1] * (1.0 / (440.0 / top).astype(BF16).astype(F32))


def first_body(high_ref, low_ref, scale_ref, block_ref, out_ref):
    out_ref[...] = product(high_ref, low_ref, scale_ref, block_ref)


def middle_body(high_ref, low_ref, scale_ref, block_ref, sum_ref, out_ref):
    out_ref[...] = sum_ref[...] + product(high_ref, low_ref, scale_ref, block_ref)


def last_body(high_ref, low_ref, scale_ref, block_ref, sum_ref, own_ref, other_ref):
    value = sum_ref[...] + product(high_ref, low_ref, scale_ref, block_ref)
    half = value.shape[0] // 2
    own_ref[...] = value[:half]
    other_ref[...] = value[half:]


def encode(value, out_ref):
    rows = value.shape[0]
    top = jnp.maximum(jnp.max(jnp.abs(value), axis=0, keepdims=True), 1e-30)
    step = jnp.ceil(16.0 * jnp.log2(top * (1.0 / 32700.0)))
    inverse = jnp.exp2(step * (-1.0 / 16.0))
    fixed = jnp.clip(jnp.round(value * inverse), -32767.0, 32767.0)
    out_ref[0:rows, :] = fixed.astype(I32).astype(I16)
    out_ref[rows:, :] = jnp.broadcast_to(step, (EXTRA, value.shape[1])).astype(I32).astype(I16)


def decode(ref):
    rows = ref.shape[0] - EXTRA
    step = ref[rows:, :].astype(I32).astype(F32)[0:1, :]
    return ref[0:rows, :].astype(I32).astype(F32) * jnp.exp2(step * (1.0 / 16.0))


def add_plain_body(a_ref, b_ref, sum_ref, code_ref):
    value = a_ref[...] + b_ref[...]
    sum_ref[...] = value
    encode(value, code_ref)


def add_coded_body(a_ref, code_in_ref, sum_ref, code_ref):
    value = a_ref[...] + decode(code_in_ref)
    sum_ref[...] = value
    encode(value, code_ref)


def add_last_body(a_ref, code_in_ref, out_ref):
    out_ref[...] = (a_ref[...] + decode(code_in_ref)).astype(BF16)


def pick_body(pick_ref, own_ref, other_ref, out_ref, far_ref):
    half = own_ref.shape[0]
    near = out_ref.shape[0]
    value = jnp.dot(pick_ref[:, 0:half], own_ref[...], preferred_element_type=F32)
    value += jnp.dot(pick_ref[:, half:], other_ref[...], preferred_element_type=F32)
    out_ref[...] = value[:near].astype(BF16)
    far_ref[...] = value[near:].astype(BF16)


def per_device(stored, integrals, layout, partner):
    rows = stored.shape[0]
    n_row, n_col = lax.axis_size("row"), lax.axis_size("col")
    line = n_row // 2
    total = rows * n_row * n_col
    pairs = total // 2
    half = pairs // 2
    depth, columns = integrals.shape
    unit, tile = depth // UNITS, columns // UNITS
    r, c = lax.axis_index("row"), lax.axis_index("col")
    z, core = r // 2, r % 2
    place = jnp.stack([z, core]).astype(I32)
    siblings = [(i, i ^ 1) for i in range(n_row)]
    chain = Chain()
    starts = [sum(CHUNKS[:i]) for i in range(len(CHUNKS))]

    def split():
        def at(i):
            return lambda u, p: (0, 2 * i + 1 - p[1])

        return chain.call(
            split_body,
            [stored] * line,
            [pl.BlockSpec((rows, depth), at(i)) for i in range(line)],
            [pl.BlockSpec((line, rows, depth), lambda u, p: (0, 0, 0))],
            [jax.ShapeDtypeStruct((line, rows, depth), BF16)],
            (1,),
            scalars=place,
        )[0]

    def stack(pieces, following):
        def whole(shape):
            return pl.BlockSpec(shape, lambda u, p: (0, 0))

        def at(step):
            return lambda u, p: (0, ((2 * lax.rem(p[0] + step, line) + p[1]) * UNITS + starts[following]) * unit)

        def other_at(step):
            return lambda u, p: (lax.rem(p[0] + step, line), 0, starts[following] * unit)

        arrays, in_specs, shapes = [], [], []
        if pieces is not None:
            rows_of, width = pieces[0].shape
            arrays += pieces
            in_specs += [whole((rows_of, width))] * line
            shapes += [(rows_of * line // 2, width)] * 2
        if following is not None:
            width = CHUNKS[following] * unit
            arrays += [stored] * line + [others] * line
            in_specs += [pl.BlockSpec((pl.Element(rows), pl.Element(width)), at(s)) for s in range(line)]
            in_specs += [pl.BlockSpec((None, pl.Element(rows), pl.Element(width)), other_at(s)) for s in range(line)]
            shapes += [(2 * rows, width)] * line
        outs = chain.call(
            stack_body(line, pieces is not None, following is not None),
            arrays,
            in_specs,
            [whole(shape) for shape in shapes],
            [jax.ShapeDtypeStruct(shape, BF16) for shape in shapes],
            (1,),
            scalars=place,
        )
        halves = outs[:2] if pieces is not None else None
        return halves, outs[2 if pieces is not None else 0 :]

    def along_z(pieces):
        out = pieces[:1]
        for step in range(1, line):
            perm = [(2 * i + k, 2 * ((i + step) % line) + k) for i in range(line) for k in range(2)]
            out.append(lax.ppermute(pieces[step], "row", perm))
        return out

    bits = [1 << b for b in range(n_col.bit_length() - 1)]
    orders = [bits, bits[::-1]]

    def over_col(halves):
        have = [[h] for h in halves]
        joined = halves
        for i in range(len(bits)):
            if i:
                width = joined[0].shape[1]
                grown = 2 * joined[0].shape[0]
                specs = [pl.BlockSpec((grown // 2, width), lambda u: (0, 0))] * 4
                joined = chain.call(
                    join_body,
                    [x for h in range(2) for x in (joined[h], have[h][-1])],
                    specs,
                    [pl.BlockSpec((grown, width), lambda u: (0, 0))] * 2,
                    [jax.ShapeDtypeStruct((grown, width), BF16)] * 2,
                    (1,),
                    vmem=32,
                )
            for h in range(2):
                perm = [(x, x ^ orders[h][i]) for x in range(n_col)]
                have[h].append(lax.ppermute(joined[h], "col", perm))
            yield
        return have[0] + have[1]

    def pair_rows(chunk, pieces):
        width = CHUNKS[chunk] * unit
        shapes = [((pairs, width), BF16), ((pairs, width), F8), ((8, 128), F32)]
        return chain.call(
            pair_rows_body,
            [select, *pieces],
            [pl.BlockSpec((pairs, total), lambda n: (0, 0))] + [pl.BlockSpec(p.shape, lambda n: (0, 0)) for p in pieces],
            [in_place(pairs, unit), in_place(pairs, unit), pl.BlockSpec((8, 128), lambda n: (0, 0))],
            [jax.ShapeDtypeStruct(shape, kind) for shape, kind in shapes],
            (CHUNKS[chunk],),
            vmem=32,
        )

    wide = WIDE * tile

    def product_specs(chunk, diff, first):
        rows_of = CHUNKS[chunk] * unit
        return [
            *[pl.BlockSpec(d.shape, lambda n: (0, 0)) for d in diff],
            pl.BlockSpec(
                (pl.Element(rows_of), pl.Element(wide)), lambda n: (starts[chunk] * unit, (first + n) * wide)
            ),
        ]

    def accumulate(chunk, diff, sums):
        in_specs = product_specs(chunk, diff, 0)
        kw = dict(
            out_specs=[in_place(pairs, wide)],
            out_shape=[jax.ShapeDtypeStruct((pairs, columns), F32)],
            grid=(columns // wide,),
            vmem=56,
        )
        if sums is None:
            return chain.call(first_body, [*diff, integrals], in_specs, **kw)[0]
        return chain.call(
            middle_body,
            [*diff, integrals, sums],
            [*in_specs, in_place(pairs, wide)],
            input_output_aliases={4: 0},
            **kw,
        )[0]

    def finish(group, diff, sums):
        first = sum(GROUPS[:group])
        return chain.call(
            last_body,
            [*diff, integrals, sums],
            [*product_specs(n - 1, diff, first), pl.BlockSpec((pairs, wide), lambda n: (0, first + n))],
            [in_place(half, wide)] * 2,
            [jax.ShapeDtypeStruct((half, GROUPS[group] * wide), F32)] * 2,
            (GROUPS[group],),
            vmem=56,
        )

    def by_columns(body, arrays, outs, first=0, units=None):
        count = arrays[-1].shape[1] // tile if units is None else units
        return chain.call(
            body,
            arrays,
            [pl.BlockSpec((a.shape[0], tile), lambda n: (0, first + n)) for a in arrays],
            [in_place(rows_of, tile) for rows_of, _ in outs],
            [jax.ShapeDtypeStruct((rows_of, count * tile), kind) for rows_of, kind in outs],
            (count,),
        )

    def row_ids():
        entries = []
        for h in range(2):
            masks = [0]
            for bit in orders[h]:
                masks += [m ^ bit for m in masks]
            for m in masks:
                for step in range(h * line // 2, (h + 1) * line // 2):
                    for flip in range(2):
                        entries += [(m, step, flip, offset) for offset in range(rows)]
        mask, step, flip, offset = np.array(entries, np.int32).T
        return ((2 * ((z - step) % line) + (core ^ flip)) * n_col + (c ^ mask)) * rows + offset

    n = len(CHUNKS)
    others = lax.ppermute(split(), "row", siblings)
    _, pieces = stack(None, 0)
    pieces = along_z(pieces)

    slab = jnp.arange(total, dtype=I32) + chain.mark[0, 0].astype(I32)
    is_first = slab < partner
    before = is_first[None, :] & (slab[None, :] < jnp.minimum(slab, partner)[:, None])
    number = jnp.sum(before.astype(I32), axis=1) + 1
    signed = jnp.where(is_first, number, -number)
    held = jnp.sum(jnp.where(slab[None, :] == layout[:, None], signed[None, :], 0), axis=1)
    held = jnp.sum(jnp.where(slab[None, :] == row_ids()[:, None], held[None, :], 0), axis=1)
    order = (jnp.arange(pairs, dtype=I32) + core * half) % pairs + 1
    select = (order[:, None] == held[None, :]).astype(BF16) - (order[:, None] == -held[None, :]).astype(BF16)
    middle = line // 2
    mine_rows = total // n_row
    outward = jnp.where(z < middle, -1, 1)
    owners = jnp.clip(z + outward * np.arange(middle, dtype=np.int32), 0, line - 1)
    wanted = (2 * jnp.repeat(owners, mine_rows) + core) * mine_rows + np.tile(np.arange(mine_rows, dtype=np.int32), middle)
    mine = jnp.sum(jnp.where(slab[None, :] == wanted[:, None], signed[None, :], 0), axis=1)
    pick = (mine[:, None] == order[None, :]).astype(BF16) - (mine[:, None] == -order[None, :]).astype(BF16)

    sums = None

    def advance(exchange):
        try:
            next(exchange)
        except StopIteration as end:
            return end.value

    halves, pieces = stack(pieces, 1)
    pieces = along_z(pieces)
    exchange = over_col(halves)
    blocks = None
    while blocks is None:
        blocks = advance(exchange)
    for i in range(1, n):
        halves, pieces = following if i > 1 else stack(pieces, i + 1 if i + 1 < n else None)
        if i + 1 < n:
            pieces = along_z(pieces)
        exchange = over_col(halves)
        advance(exchange)
        diff = pair_rows(i - 1, blocks)
        blocks = None
        while blocks is None:
            blocks = advance(exchange)
        sums = accumulate(i - 1, diff, sums)
        if i + 1 < n:
            following = stack(pieces, i + 2 if i + 2 < n else None)
    diff = pair_rows(n - 1, blocks)

    def along(pairs_of_z):
        return [(2 * a + k, 2 * b + k) for a, b in pairs_of_z for k in range(2)]

    groups = [None] * len(GROUPS)

    def send(group):
        own, foreign = groups[group]
        anywhere = pl.BlockSpec(memory_space=pl.ANY)
        shape = jax.ShapeDtypeStruct(foreign.shape, foreign.dtype)
        if group:
            (foreign,) = chain.call(
                lambda *refs: None, [foreign], [anywhere], [anywhere], [shape], (1,), input_output_aliases={0: 0}
            )
        groups[group] = [own, lax.ppermute(foreign, "row", siblings)]

    def begin(part):
        group, first, units = PARTS[part]
        return groups[group], first, units

    def inward(step, state):
        outs = [(half, F32), (half + EXTRA, I16)]
        if step == 0:
            value, code = by_columns(add_plain_body, state[0], outs, state[1], state[2])
        else:
            value, code = by_columns(add_coded_body, list(state), outs)
        if step < middle - 1:
            perm = along([(step, step + 1), (line - 1 - step, line - 2 - step)])
        else:
            perm = along([(middle - 1, middle), (middle, middle - 1)])
        return value, lax.ppermute(code, "row", perm)

    def whole(state):
        (done,) = by_columns(add_last_body, list(state), [(half, BF16)])
        return done, lax.ppermute(done, "row", siblings)

    def spread(state):
        width = state[0].shape[1]
        far = (middle - 1) * mine_rows
        own, rest = chain.call(
            pick_body,
            [pick, *state],
            [pl.BlockSpec(pick.shape, lambda n: (0, 0)), in_place(half, tile), in_place(half, tile)],
            [in_place(mine_rows, tile), in_place(far, tile)],
            [jax.ShapeDtypeStruct((mine_rows, width), BF16), jax.ShapeDtypeStruct((far, width), BF16)],
            (width // tile,),
        )
        distance = jnp.where(z < middle, middle - 1 - z, z - middle)
        for step in range(middle - 1):
            perm = along([(middle - 1 - step, middle - 2 - step), (middle + step, middle + 1 + step)])
            rest = lax.ppermute(rest, "row", perm)
            own = jnp.where(distance == step + 1, rest[:mine_rows], own)
            rest = rest[mine_rows:]
        return own

    stages = [lambda s, k=k: inward(k, s) for k in range(middle)] + [whole, spread]
    state = [None] * len(PARTS)
    for stage, item in ORDER if len(stages) == 4 else (
        [(k, g) for k in (0, 1) for g in range(len(GROUPS))]
        + sorted(
            ((k + 2, p) for p in range(len(PARTS)) for k in range(len(stages))), key=lambda x: (x[0] + x[1], x[0])
        )
    ):
        if stage == 0:
            groups[item] = finish(item, diff, sums)
        elif stage == 1:
            send(item)
        else:
            state[item] = stages[stage - 2](begin(item) if stage == 2 else state[item])
    return jnp.concatenate(state, axis=1)


def solution(mesh):
    return jax.shard_map(
        per_device,
        mesh=mesh,
        in_specs=(P(("row", "col"), None), P("row", "col"), P(), P()),
        out_specs=P("row", "col"),
        check_vma=False,
    )
```
